32 devices in a mesh: band: 8 (over z, y), chan: 4 (over x, core).
Axes of the slice: x: 2, y: 2, z: 4, core: 2. Of those that a mesh axis runs over, the one named last changes fastest.
Arguments:
- new_frames: bfloat16 [4, 32, 512, 320], P(None, 'band', 'chan'), may hold values from -6 to 6
- cached_frames: bfloat16 [2, 32, 512, 320], P(None, 'band', 'chan'), may hold values from -6 to 6
- conv_weight: bfloat16 [3, 3, 3, 512, 512], P(None, None, None, 'chan'), may hold values from -0.0546875 to 0.0546875
- out_bias: float32 [512], P('chan'), may hold values from -3 to 3
Outputs:
- conv_out: bfloat16 [4, 32, 512, 320], P(None, 'band', 'chan')
The draws below stay inside these ranges and needn't reach their ends.
All inputs are finite; a program needn't handle non-finite values.
Results may differ from the reference program's by a relative error of at most 0.001.
Values may be sent and summed in bfloat16 or wider, within the bound.
A program may use at most 128 MiB of HBM per device.

```python
import jax
import jax.numpy as jnp

C = 512
W = 320
FRAMES = 4
CACHE = 2
H = 32


def shard_levels(rng, extent, shards, least, top_value):
    level, own = 1.0, jax.random.fold_in(rng, 6)
    for axis_at, shards_of in shards:
        steps = jnp.exp(jax.random.uniform(jax.random.fold_in(own, axis_at), (shards_of,), jnp.float32, least / len(shards), top_value / len(shards)))
        level = level * jnp.repeat(steps, extent[axis_at] // shards_of).reshape([-1 if axis == axis_at else 1 for axis in range(len(extent))])
    return level


def scatter_about(own_key, shape, deviation, reach, shards=(), dtype=jnp.bfloat16):
    values = jax.random.normal(own_key, shape, jnp.float32) * deviation
    if len(shards) > 0:
        values = shard_levels(own_key, shape, shards, -0.22, 0.18) * values
    return jnp.clip(values, min=-reach, max=reach).astype(dtype)


def setup_inputs(seed: int = 0) -> dict:
    key_list = jax.random.split(jax.random.key(seed), 5)
    return {
        "new_frames": scatter_about(key_list[0], (FRAMES, H, C, W), 1.0, 6.0, ((1, 8), (2, 4))),
        "cached_frames": scatter_about(key_list[1], (CACHE, H, C, W), 1.0, 6.0, ((1, 8), (2, 4))),
        "conv_weight": scatter_about(key_list[2], (3, 3, 3, C, C), (27 * C) ** -0.5, 0.0546875, ((3, 4),)),
        "out_bias": scatter_about(key_list[3], (C,), 0.5, 3.0, ((0, 4),), jnp.float32),
    }


def reference(new_frames, cached_frames, conv_weight, out_bias):
    stacked = jnp.concatenate([cached_frames, new_frames], axis=0).astype(jnp.float32)
    padded = jnp.pad(stacked, ((0, 0), (1, 1), (0, 0), (1, 1)))
    weights_wide = conv_weight.astype(jnp.float32)
    frame_count = new_frames.shape[0]
    row_count = new_frames.shape[1]
    col_count = new_frames.shape[3]
    summed = jnp.zeros((frame_count, row_count, conv_weight.shape[3], col_count), jnp.float32)
    for time_tap in range(3):
        for row_tap in range(3):
            for col_tap in range(3):
                window = padded[time_tap:time_tap + frame_count, row_tap:row_tap + row_count, :, col_tap:col_tap + col_count]
                summed = summed + jnp.einsum("dc,frcw->frdw", weights_wide[time_tap, row_tap, col_tap], window)
    return (summed + out_bias.astype(jnp.float32)[None, None, :, None]).astype(jnp.bfloat16)
```

```python
import functools

import jax
import jax.numpy as jnp
from jax import lax
from jax.experimental import pallas as pl
from jax.experimental.pallas import tpu as pltpu
from jax.sharding import PartitionSpec as P

MESH = pl.DeviceIdType.MESH
LANES = 128
CORES = 2


def conv_kernel(
    dims, cached_ref, new_ref, w_ref, bias_ref, out_ref,
    xb, hb, wb, acc, obuf,
    local_sem, weight_sem, out_sem,
    peer_send, peer_recv, sib_send, sib_recv,
    edge_send, edge_recv, fwd_send, fwd_recv,
):
    bands, chans, cached, outs, depth, width, row_count = dims
    frames = cached + outs
    chips = chans // CORES
    band, chan = lax.axis_index("band"), lax.axis_index("chan")
    chip, core = chan // CORES, chan % CORES
    sibling = {"chan": chip * CORES + (1 - core)}
    has_above, has_below = band > 0, band < bands - 1
    sides = ((0, has_above, {"band": band - 1}), (1, has_below, {"band": band + 1}))

    def peer(step):
        return {"chan": lax.rem(chip + step, chips) * CORES + core}

    def own(f):
        return cached_ref.at[f] if f < cached else new_ref.at[f - cached]

    def remote(src, dst, send, recv, device):
        return pltpu.make_async_remote_copy(
            src_ref=src, dst_ref=dst, send_sem=send, recv_sem=recv,
            device_id=device, device_id_type=MESH,
        )

    def weight_copy(slot, t):
        owner = lax.rem(chip + chips - slot, chips)
        span = CORES * depth
        return pltpu.make_async_copy(
            w_ref.at[t, :, pl.ds(pl.multiple_of(owner * span, LANES), span)],
            wb.at[slot, :, pl.ds(t * span, span)],
            weight_sem.at[slot, t],
        )

    def local_copy(f):
        return pltpu.make_async_copy(own(f), xb.at[0, f, core], local_sem.at[f])

    def peer_copy(step, f):
        return remote(
            own(f), xb.at[step, f, core],
            peer_send.at[step, f], peer_recv.at[step, f], peer(step),
        )

    def sib_copy(slot, f):
        src = own(f) if slot == 0 else xb.at[slot, f, core]
        return remote(
            src, xb.at[slot, f, core], sib_send.at[slot, f], sib_recv.at[slot, f], sibling
        )

    def edge_copy(slot, f, side):
        part = pl.ds(0 if side == 0 else (row_count - 1) * width, width)
        src = own(f).at[part] if slot == 0 else xb.at[slot, f, core, part]
        return remote(
            src, hb.at[slot, 1 - side, f, core],
            edge_send.at[slot, side, f], edge_recv.at[slot, 1 - side, f], sides[side][2],
        )

    def fwd_copy(slot, f, rim):
        ref = hb.at[slot, rim, f, core]
        return remote(ref, ref, fwd_send.at[slot, rim, f], fwd_recv.at[slot, rim, f], sibling)

    def each_side(act):
        for side, there, device in sides:
            pl.when(there)(functools.partial(act, side, device))

    def start_edges(slot, f):
        each_side(lambda side, _: edge_copy(slot, f, side).start())

    barrier = pltpu.get_barrier_semaphore()

    def greet(device):
        pl.semaphore_signal(barrier, inc=1, device_id=device, device_id_type=MESH)

    greet(sibling)
    for step in range(1, chips):
        greet(peer(step))
    each_side(lambda _, device: greet(device))
    for slot in range(chips):
        for t in range(3):
            weight_copy(slot, t).start()
    for f in range(frames):
        local_copy(f).start()
    pl.semaphore_wait(barrier, chips + has_above.astype(jnp.int32) + has_below.astype(jnp.int32))

    ahead = 2
    for f in range(ahead):
        for step in range(1, chips):
            peer_copy(step, f).start()
    for f in range(frames):
        sib_copy(0, f).start()
    for f in range(frames):
        start_edges(0, f)

    for rim, there, _ in sides:
        @pl.when(jnp.logical_not(there))
        def _(rim=rim):
            hb[:, rim] = jnp.zeros((hb.shape[0],) + hb.shape[2:], hb.dtype)

    @pl.loop(0, outs * row_count)
    def _(n):
        at = pl.ds(pl.multiple_of(n * width, width), width)
        for j in range(3):
            start = bias_ref[...] if j == 1 else jnp.zeros_like(bias_ref)
            acc[at, j * depth : (j + 1) * depth] = jnp.broadcast_to(start, (width, depth))

    def serve(f):
        for step in range(1, chips):
            peer_copy(step, f).wait_recv()
            sib_copy(step, f).start()
            start_edges(step, f)
            peer_copy(step, f).wait_send()
            if f + ahead < frames:
                peer_copy(step, f + ahead).start()

    def serve_edges(slot, f):
        def act(rim, _):
            edge_copy(slot, f, 1 - rim).wait_recv()
            fwd_copy(slot, f, rim).start()

        each_side(act)

    def wait_rims(slot, f):
        each_side(lambda rim, _: fwd_copy(slot, f, rim).wait_recv())

    def add(slot, f, pieces, row, taps):
        lo, hi = taps
        group = 3 * depth
        product = lax.dot_general(
            jnp.concatenate(pieces, axis=1),
            wb[slot, lo * group : (hi + 1) * group, :],
            (((1,), (1,)), ((), ())),
            preferred_element_type=jnp.float32,
        )
        for i in range(lo, hi + 1):
            start = (f * row_count + row + 1 - i) * width
            at = pl.ds(start if isinstance(row, int) else pl.multiple_of(start, width), width)
            acc[at, :] = acc[at, :] + product[:, (i - lo) * group : (i - lo + 1) * group]

    def accumulate(slot, f):
        def add_row(row, taps):
            start = row * width
            at = pl.ds(start if isinstance(row, int) else pl.multiple_of(start, width), width)
            add(
                slot, f, [xb[slot, f + t, c, at, :] for t in range(3) for c in range(CORES)],
                row, taps,
            )

        add_row(0, (0, 1))
        add_row(row_count - 1, (1, 2))
        pl.loop(1, row_count - 1)(lambda row: add_row(row, (0, 2)))

    def accumulate_rims(slot, f):
        for rim, row in ((0, -1), (1, row_count)):
            add(
                slot, f, [hb[slot, rim, f + t, c] for t in range(3) for c in range(CORES)],
                row, (2 * rim, 2 * rim),
            )

    def finish(f):
        column = lax.broadcasted_iota(jnp.int32, (width, depth), 0)

        @pl.loop(0, row_count)
        def _(row):
            at = pl.ds(pl.multiple_of((f * row_count + row) * width, width), width)
            left = pltpu.roll(acc[at, 0:depth], 1, 0)
            right = pltpu.roll(acc[at, 2 * depth : 3 * depth], width - 1, 0)
            total = acc[at, depth : 2 * depth]
            total = total + jnp.where(column == 0, 0.0, left)
            total = total + jnp.where(column == width - 1, 0.0, right)
            obuf[f, pl.ds(pl.multiple_of(row * width, width), width), :] = total.astype(obuf.dtype)

        out_copy(f).start()

    def out_copy(f):
        return pltpu.make_async_copy(obuf.at[f], out_ref.at[f], out_sem.at[f])

    for t in range(3):
        weight_copy(0, t).wait()
    for f in range(outs):
        for g in range(3) if f == 0 else (f + 2,):
            local_copy(g).wait()
            sib_copy(0, g).wait_recv()
        accumulate(0, f)
    for slot in range(1, chips):
        for t in range(3):
            weight_copy(slot, t).wait()

    serve(0)
    serve(1)
    for f in range(frames):
        serve_edges(0, f)
    for f in range(2, frames):
        serve(f)
        for step in range(1, chips):
            for g in (0, 1) if f == 2 else (f - 1,):
                serve_edges(step, g)
            for g in (0, 1, 2) if f == 2 else (f,):
                sib_copy(step, g).wait_recv()
            accumulate(step, f - 2)
        if f == 3:
            for g in range(frames):
                wait_rims(0, g)
            for o in range(outs):
                accumulate_rims(0, o)
        if f >= 3:
            for step in range(1, chips):
                for g in (0, 1, 2) if f == 3 else (f - 1,):
                    wait_rims(step, g)
                accumulate_rims(step, f - 3)
            finish(f - 3)
    for step in range(1, chips):
        serve_edges(step, frames - 1)
        wait_rims(step, frames - 1)
        accumulate_rims(step, outs - 1)
    finish(outs - 1)

    for f in range(frames):
        for slot in range(chips):
            sib_copy(slot, f).wait_send()

            def gone(side, _, slot=slot, f=f):
                edge_copy(slot, f, side).wait_send()
                fwd_copy(slot, f, side).wait_send()

            each_side(gone)
    for f in range(outs):
        out_copy(f).wait()


def on_device(bands, chans, new_frames, cached_frames, conv_weight, out_bias):
    outs, row_count, own_depth, width = new_frames.shape
    cached = cached_frames.shape[0]
    frames = cached + outs
    chips = chans // CORES
    depth = -(-own_depth // LANES) * LANES
    extra = depth - own_depth

    def rows_first(block):
        block = block.transpose(0, 1, 3, 2).reshape(block.shape[0], row_count * width, own_depth)
        return jnp.pad(block, ((0, 0), (0, 0), (0, extra)))

    weights = conv_weight.reshape(3, 9, own_depth, chans, own_depth)
    weights = jnp.pad(weights, ((0, 0), (0, 0), (0, extra), (0, 0), (0, extra)))
    weights = weights.reshape(3, 9 * depth, chans * depth)
    dims = (bands, chans, cached, outs, depth, width, row_count)
    sem = pltpu.SemaphoreType.DMA
    positions = row_count * width
    result = pl.pallas_call(
        functools.partial(conv_kernel, dims),
        out_shape=jax.ShapeDtypeStruct((outs, positions, depth), jnp.bfloat16),
        in_specs=[
            pl.BlockSpec(memory_space=pl.ANY),
            pl.BlockSpec(memory_space=pl.ANY),
            pl.BlockSpec(memory_space=pl.ANY),
            pl.BlockSpec(memory_space=pltpu.VMEM),
        ],
        out_specs=pl.BlockSpec(memory_space=pl.ANY),
        scratch_shapes=[
            pltpu.VMEM((chips, frames, CORES, positions, depth), jnp.bfloat16),
            pltpu.VMEM((chips, 2, frames, CORES, width, depth), jnp.bfloat16),
            pltpu.VMEM((chips, 9 * depth, 3 * CORES * depth), jnp.bfloat16),
            pltpu.VMEM((outs * positions, 3 * depth), jnp.float32),
            pltpu.VMEM((outs, positions, depth), jnp.bfloat16),
            sem((frames,)),
            sem((chips, 3)),
            sem((outs,)),
            sem((chips, frames)),
            sem((chips, frames)),
            sem((chips, frames)),
            sem((chips, frames)),
            sem((chips, 2, frames)),
            sem((chips, 2, frames)),
            sem((chips, 2, frames)),
            sem((chips, 2, frames)),
        ],
        compiler_params=pltpu.CompilerParams(
            collective_id=0, has_side_effects=True, vmem_limit_bytes=56 * 2**20
        ),
        cost_estimate=pl.CostEstimate(
            flops=2 * 27 * outs * positions * depth * chans * depth,
            bytes_accessed=2 * (weights.size + (frames + outs) * positions * depth),
            transcendentals=0,
        ),
    )(
        rows_first(cached_frames), rows_first(new_frames), weights,
        jnp.pad(out_bias, (0, extra))[None, :],
    )
    result = result[:, :, :own_depth].reshape(outs, row_count, width, own_depth)
    return result.transpose(0, 1, 3, 2)


def solution(mesh):
    in_specs = (
        P(None, "band", "chan", None),
        P(None, "band", "chan", None),
        P(None, None, None, "chan", None),
        P("chan"),
    )
    out_specs = P(None, "band", "chan", None)
    return jax.shard_map(
        functools.partial(on_device, mesh.shape["band"], mesh.shape["chan"]),
        mesh=mesh, in_specs=in_specs, out_specs=out_specs, check_vma=False,
    )
```

```python
import functools

import jax
import jax.numpy as jnp
from jax import lax
from jax.experimental import pallas as pl
from jax.experimental.pallas import tpu as pltpu
from jax.sharding import PartitionSpec as P

MESH = pl.DeviceIdType.MESH
LANES = 128
CORES = 2


def conv_kernel(
    dims, cached_ref, new_ref, w_ref, bias_ref, out_ref,
    xb, hb, wb, acc, obuf,
    local_sem, weight_sem, out_sem,
    peer_send, peer_recv, sib_send, sib_recv,
    edge_send, edge_recv, fwd_send, fwd_recv,
):
    bands, chans, cached, outs, depth, width, row_count = dims
    frames = cached + outs
    chips = chans // CORES
    band, chan = lax.axis_index("band"), lax.axis_index("chan")
    chip, core = chan // CORES, chan % CORES
    sibling = {"chan": chip * CORES + (1 - core)}
    has_above, has_below = band > 0, band < bands - 1
    sides = ((0, has_above, {"band": band - 1}), (1, has_below, {"band": band + 1}))

    def peer(step):
        return {"chan": lax.rem(chip + step, chips) * CORES + core}

    def own(f):
        return cached_ref.at[f] if f < cached else new_ref.at[f - cached]

    def remote(src, dst, send, recv, device):
        return pltpu.make_async_remote_copy(
            src_ref=src, dst_ref=dst, send_sem=send, recv_sem=recv,
            device_id=device, device_id_type=MESH,
        )

    def weight_copy(slot, t):
        owner = lax.rem(chip + chips - slot, chips)
        span = CORES * depth
        return pltpu.make_async_copy(
            w_ref.at[t, :, pl.ds(pl.multiple_of(owner * span, LANES), span)],
            wb.at[slot, :, pl.ds(t * span, span)],
            weight_sem.at[slot, t],
        )

    def local_copy(f):
        return pltpu.make_async_copy(own(f), xb.at[0, f, core], local_sem.at[f])

    FIRST, LAST, MIDDLE = range(3)
    spans = (
        pl.ds(0, width),
        pl.ds((row_count - 1) * width, width),
        pl.ds(width, (row_count - 2) * width),
    )

    def peer_copy(step, f, part):
        return remote(
            own(f).at[spans[part]], xb.at[step, f, core, spans[part]],
            peer_send.at[step, part, f], peer_recv.at[step, part, f], peer(step),
        )

    def own_copy(f):
        return remote(
            own(f), xb.at[0, f, core], sib_send.at[0, 0, f], sib_recv.at[0, 0, f], sibling
        )

    def sib_copy(step, f, part):
        ref = xb.at[step, f, core, spans[part]]
        return remote(ref, ref, sib_send.at[step, part, f], sib_recv.at[step, part, f], sibling)

    def edge_copy(slot, f, side):
        span = spans[FIRST if side == 0 else LAST]
        src = own(f).at[span] if slot == 0 else xb.at[slot, f, core, span]
        return remote(
            src, hb.at[slot, 1 - side, f, core],
            edge_send.at[slot, side, f], edge_recv.at[slot, 1 - side, f], sides[side][2],
        )

    def fwd_copy(slot, f, rim):
        ref = hb.at[slot, rim, f, core]
        return remote(ref, ref, fwd_send.at[slot, rim, f], fwd_recv.at[slot, rim, f], sibling)

    def each_side(act):
        for side, there, device in sides:
            pl.when(there)(functools.partial(act, side, device))

    def start_edges(slot, f):
        each_side(lambda side, _: edge_copy(slot, f, side).start())

    barrier = pltpu.get_barrier_semaphore()

    def greet(device):
        pl.semaphore_signal(barrier, inc=1, device_id=device, device_id_type=MESH)

    greet(sibling)
    for step in range(1, chips):
        greet(peer(step))
    each_side(lambda _, device: greet(device))
    for slot in range(chips):
        for t in range(3):
            weight_copy(slot, t).start()
    for f in range(frames):
        local_copy(f).start()
    pl.semaphore_wait(barrier, chips + has_above.astype(jnp.int32) + has_below.astype(jnp.int32))

    ahead = 4
    queue = [(f, (FIRST, LAST)) for f in range(frames)] + [(f, (MIDDLE,)) for f in range(frames)]

    def send(place):
        f, parts = queue[place]
        for step in range(1, chips):
            for part in parts:
                peer_copy(step, f, part).start()

    for place in range(ahead):
        send(place)
    for f in range(frames):
        own_copy(f).start()
    for f in range(frames):
        start_edges(0, f)

    for rim, there, _ in sides:
        @pl.when(jnp.logical_not(there))
        def _(rim=rim):
            hb[:, rim] = jnp.zeros((hb.shape[0],) + hb.shape[2:], hb.dtype)

    @pl.loop(0, outs * row_count)
    def _(n):
        at = pl.ds(pl.multiple_of(n * width, width), width)
        for j in range(3):
            start = bias_ref[...] if j == 1 else jnp.zeros_like(bias_ref)
            acc[at, j * depth : (j + 1) * depth] = jnp.broadcast_to(start, (width, depth))

    def serve(place):
        f, parts = queue[place]
        for step in range(1, chips):
            for part in parts:
                peer_copy(step, f, part).wait_recv()
                sib_copy(step, f, part).start()
            if FIRST in parts:
                start_edges(step, f)
        for step in range(1, chips):
            for part in parts:
                peer_copy(step, f, part).wait_send()
        if place + ahead < len(queue):
            send(place + ahead)

    def serve_edges(slot, f):
        def act(rim, _):
            edge_copy(slot, f, 1 - rim).wait_recv()
            fwd_copy(slot, f, rim).start()

        each_side(act)

    def wait_rims(slot, f):
        each_side(lambda rim, _: fwd_copy(slot, f, rim).wait_recv())

    def add(slot, f, ref_of, times, row, taps):
        lo, hi = taps
        group, span = 3 * depth, CORES * depth
        product = lax.dot_general(
            jnp.concatenate([ref_of(f + t, c) for t in times for c in range(CORES)], axis=1),
            wb[slot, lo * group : (hi + 1) * group, times[0] * span : (times[-1] + 1) * span],
            (((1,), (1,)), ((), ())),
            preferred_element_type=jnp.float32,
        )
        for i in range(lo, hi + 1):
            start = (f * row_count + row + 1 - i) * width
            at = pl.ds(start if isinstance(row, int) else pl.multiple_of(start, width), width)
            acc[at, :] = acc[at, :] + product[:, (i - lo) * group : (i - lo + 1) * group]

    every = (0, 1, 2)

    def add_row(slot, f, row, taps, times=every):
        start = row * width
        at = pl.ds(start if isinstance(row, int) else pl.multiple_of(start, width), width)
        add(slot, f, lambda g, c: xb[slot, g, c, at, :], times, row, taps)

    def add_edges(slot, f):
        add_row(slot, f, 0, (0, 1))
        add_row(slot, f, row_count - 1, (1, 2))

    def add_middle(slot, f, times=every):
        pl.loop(1, row_count - 1)(lambda row: add_row(slot, f, row, (0, 2), times))

    def add_rims(slot, f, times=every):
        for rim, row in ((0, -1), (1, row_count)):
            add(
                slot, f, lambda g, c, rim=rim: hb[slot, rim, g, c], times,
                row, (2 * rim, 2 * rim),
            )

    def finish(f):
        column = lax.broadcasted_iota(jnp.int32, (width, depth), 0)

        @pl.loop(0, row_count)
        def _(row):
            at = pl.ds(pl.multiple_of((f * row_count + row) * width, width), width)
            left = pltpu.roll(acc[at, 0:depth], 1, 0)
            right = pltpu.roll(acc[at, 2 * depth : 3 * depth], width - 1, 0)
            total = acc[at, depth : 2 * depth]
            total = total + jnp.where(column == 0, 0.0, left)
            total = total + jnp.where(column == width - 1, 0.0, right)
            obuf[f, pl.ds(pl.multiple_of(row * width, width), width), :] = total.astype(obuf.dtype)

        out_copy(f).start()

    def out_copy(f):
        return pltpu.make_async_copy(obuf.at[f], out_ref.at[f], out_sem.at[f])

    others = range(1, chips)

    def wait_sibling(f, parts):
        for step in others:
            for part in parts:
                sib_copy(step, f, part).wait_recv()

    for t in range(3):
        weight_copy(0, t).wait()
    for f in range(outs):
        for g in range(3) if f == 0 else (f + 2,):
            local_copy(g).wait()
            own_copy(g).wait_recv()
        add_edges(0, f)
        add_middle(0, f)
        serve(f)
    for slot in others:
        for t in range(3):
            weight_copy(slot, t).wait()
    for place in range(outs, frames):
        serve(place)
    for f in range(frames):
        serve_edges(0, f)
        wait_sibling(f, (FIRST, LAST))
    for f in range(outs):
        for step in others:
            add_edges(step, f)
        if f % 2 == 1:
            serve(frames + f // 2)
    for f in range(frames):
        wait_rims(0, f)
    for f in range(outs):
        add_rims(0, f)
    for f in range(2, frames):
        serve(frames + f)
        last = f == frames - 1
        for step in others:
            for g in (0, 1, 2) if f == 2 else (f,):
                serve_edges(step, g)
        for g in (0, 1, 2) if f == 2 else (f,):
            wait_sibling(g, (MIDDLE,))
        for step in others:
            add_middle(step, f - 2, (2,) if last else every)
            for g in (0, 1, 2) if f == 2 else (f,):
                wait_rims(step, g)
            add_rims(step, f - 2, (2,) if last else every)
        finish(f - 2)
        if f == frames - 2:
            for step in others:
                add_middle(step, outs - 1, (0, 1))
                add_rims(step, outs - 1, (0, 1))

    for f in range(frames):
        own_copy(f).wait_send()
        for slot in range(chips):
            for part in range(3) if slot > 0 else ():
                sib_copy(slot, f, part).wait_send()

            def gone(side, _, slot=slot, f=f):
                edge_copy(slot, f, side).wait_send()
                fwd_copy(slot, f, side).wait_send()

            each_side(gone)
    for f in range(outs):
        out_copy(f).wait()


def on_device(bands, chans, new_frames, cached_frames, conv_weight, out_bias):
    outs, row_count, own_depth, width = new_frames.shape
    cached = cached_frames.shape[0]
    frames = cached + outs
    chips = chans // CORES
    depth = -(-own_depth // LANES) * LANES
    extra = depth - own_depth

    def rows_first(block):
        block = block.transpose(0, 1, 3, 2).reshape(block.shape[0], row_count * width, own_depth)
        return jnp.pad(block, ((0, 0), (0, 0), (0, extra)))

    weights = conv_weight.reshape(3, 9, own_depth, chans, own_depth)
    weights = jnp.pad(weights, ((0, 0), (0, 0), (0, extra), (0, 0), (0, extra)))
    weights = weights.reshape(3, 9 * depth, chans * depth)
    dims = (bands, chans, cached, outs, depth, width, row_count)
    sem = pltpu.SemaphoreType.DMA
    positions = row_count * width
    result = pl.pallas_call(
        functools.partial(conv_kernel, dims),
        out_shape=jax.ShapeDtypeStruct((outs, positions, depth), jnp.bfloat16),
        in_specs=[
            pl.BlockSpec(memory_space=pl.ANY),
            pl.BlockSpec(memory_space=pl.ANY),
            pl.BlockSpec(memory_space=pl.ANY),
            pl.BlockSpec(memory_space=pltpu.VMEM),
        ],
        out_specs=pl.BlockSpec(memory_space=pl.ANY),
        scratch_shapes=[
            pltpu.VMEM((chips, frames, CORES, positions, depth), jnp.bfloat16),
            pltpu.VMEM((chips, 2, frames, CORES, width, depth), jnp.bfloat16),
            pltpu.VMEM((chips, 9 * depth, 3 * CORES * depth), jnp.bfloat16),
            pltpu.VMEM((outs * positions, 3 * depth), jnp.float32),
            pltpu.VMEM((outs, positions, depth), jnp.bfloat16),
            sem((frames,)),
            sem((chips, 3)),
            sem((outs,)),
            sem((chips, 3, frames)),
            sem((chips, 3, frames)),
            sem((chips, 3, frames)),
            sem((chips, 3, frames)),
            sem((chips, 2, frames)),
            sem((chips, 2, frames)),
            sem((chips, 2, frames)),
            sem((chips, 2, frames)),
        ],
        compiler_params=pltpu.CompilerParams(
            collective_id=0, has_side_effects=True, vmem_limit_bytes=56 * 2**20
        ),
        cost_estimate=pl.CostEstimate(
            flops=2 * 27 * outs * positions * depth * chans * depth,
            bytes_accessed=2 * (weights.size + (frames + outs) * positions * depth),
            transcendentals=0,
        ),
    )(
        rows_first(cached_frames), rows_first(new_frames), weights,
        jnp.pad(out_bias, (0, extra))[None, :],
    )
    result = result[:, :, :own_depth].reshape(outs, row_count, width, own_depth)
    return result.transpose(0, 1, 3, 2)


def solution(mesh):
    in_specs = (
        P(None, "band", "chan", None),
        P(None, "band", "chan", None),
        P(None, None, None, "chan", None),
        P("chan"),
    )
    out_specs = P(None, "band", "chan", None)
    return jax.shard_map(
        functools.partial(on_device, mesh.shape["band"], mesh.shape["chan"]),
        mesh=mesh, in_specs=in_specs, out_specs=out_specs, check_vma=False,
    )
```

```python
import functools

import jax
import jax.numpy as jnp
from jax import lax
from jax.experimental import pallas as pl
from jax.experimental.pallas import tpu as pltpu
from jax.sharding import PartitionSpec as P

MESH = pl.DeviceIdType.MESH
LANES = 128
CORES = 2


def conv_kernel(
    dims, cached_ref, new_ref, w_ref, bias_ref, out_ref,
    xb, hb, wb, wt, acc, obuf,
    local_sem, weight_sem, out_sem,
    peer_send, peer_recv, sib_send, sib_recv,
    edge_send, edge_recv, fwd_send, fwd_recv,
):
    bands, chans, cached, outs, depth, width, row_count = dims
    frames = cached + outs
    chips = chans // CORES
    band, chan = lax.axis_index("band"), lax.axis_index("chan")
    chip, core = chan // CORES, chan % CORES
    sibling = {"chan": chip * CORES + (1 - core)}
    has_above, has_below = band > 0, band < bands - 1
    sides = ((0, has_above, {"band": band - 1}), (1, has_below, {"band": band + 1}))

    def peer(step):
        return {"chan": lax.rem(chip + step, chips) * CORES + core}

    def turn_weights(slot):
        for t in range(3):
            weight_copy(slot, t).wait()

        @pl.loop(0, 9)
        def _(n):
            at = pl.ds(pl.multiple_of(n * depth, depth), depth)
            wt[slot, :, at] = wb[slot, at, :].T

    def own(f):
        return cached_ref.at[f] if f < cached else new_ref.at[f - cached]

    def remote(src, dst, send, recv, device):
        return pltpu.make_async_remote_copy(
            src_ref=src, dst_ref=dst, send_sem=send, recv_sem=recv,
            device_id=device, device_id_type=MESH,
        )

    def weight_copy(slot, t):
        owner = lax.rem(chip + chips - slot, chips)
        span = CORES * depth
        return pltpu.make_async_copy(
            w_ref.at[t, :, pl.ds(pl.multiple_of(owner * span, LANES), span)],
            wb.at[slot, :, pl.ds(t * span, span)],
            weight_sem.at[slot, t],
        )

    def local_copy(f):
        return pltpu.make_async_copy(own(f), xb.at[0, f, core], local_sem.at[f])

    FIRST, LAST, MIDDLE = range(3)
    spans = (
        pl.ds(0, width),
        pl.ds((row_count - 1) * width, width),
        pl.ds(width, (row_count - 2) * width),
    )

    def peer_copy(step, f, part):
        return remote(
            own(f).at[spans[part]], xb.at[step, f, core, spans[part]],
            peer_send.at[step, part, f], peer_recv.at[step, part, f], peer(step),
        )

    def own_copy(f):
        return remote(
            own(f), xb.at[0, f, core], sib_send.at[0, 0, f], sib_recv.at[0, 0, f], sibling
        )

    def sib_copy(step, f, part):
        ref = xb.at[step, f, core, spans[part]]
        return remote(ref, ref, sib_send.at[step, part, f], sib_recv.at[step, part, f], sibling)

    def edge_copy(slot, f, side):
        span = spans[FIRST if side == 0 else LAST]
        src = own(f).at[span] if slot == 0 else xb.at[slot, f, core, span]
        return remote(
            src, hb.at[slot, 1 - side, f, core],
            edge_send.at[slot, side, f], edge_recv.at[slot, 1 - side, f], sides[side][2],
        )

    def fwd_copy(slot, f, rim):
        ref = hb.at[slot, rim, f, core]
        return remote(ref, ref, fwd_send.at[slot, rim, f], fwd_recv.at[slot, rim, f], sibling)

    def each_side(act):
        for side, there, device in sides:
            pl.when(there)(functools.partial(act, side, device))

    def start_edges(slot, f):
        each_side(lambda side, _: edge_copy(slot, f, side).start())

    barrier = pltpu.get_barrier_semaphore()

    def greet(device):
        pl.semaphore_signal(barrier, inc=1, device_id=device, device_id_type=MESH)

    greet(sibling)
    for step in range(1, chips):
        greet(peer(step))
    each_side(lambda _, device: greet(device))
    for slot in range(chips):
        for t in range(3):
            weight_copy(slot, t).start()
    for f in range(frames):
        local_copy(f).start()
    pl.semaphore_wait(barrier, chips + has_above.astype(jnp.int32) + has_below.astype(jnp.int32))

    ahead = 4
    queue = [(f, (FIRST, LAST)) for f in range(frames)] + [(f, (MIDDLE,)) for f in range(frames)]

    def send(place):
        f, parts = queue[place]
        for step in range(1, chips):
            for part in parts:
                peer_copy(step, f, part).start()

    for place in range(ahead):
        send(place)
    for f in range(frames):
        own_copy(f).start()
    for f in range(frames):
        start_edges(0, f)

    for rim, there, _ in sides:
        @pl.when(jnp.logical_not(there))
        def _(rim=rim):
            hb[:, rim] = jnp.zeros((hb.shape[0],) + hb.shape[2:], hb.dtype)

    @pl.loop(0, outs * row_count)
    def _(n):
        at = pl.ds(pl.multiple_of(n * width, width), width)
        for j in range(3):
            start = bias_ref[...] if j == 1 else jnp.zeros_like(bias_ref)
            acc[at, j * depth : (j + 1) * depth] = jnp.broadcast_to(start, (width, depth))

    def serve(place):
        f, parts = queue[place]
        for step in range(1, chips):
            for part in parts:
                peer_copy(step, f, part).wait_recv()
                sib_copy(step, f, part).start()
            if FIRST in parts:
                start_edges(step, f)
        for step in range(1, chips):
            for part in parts:
                peer_copy(step, f, part).wait_send()
        if place + ahead < len(queue):
            send(place + ahead)

    def serve_edges(slot, f):
        def act(rim, _):
            edge_copy(slot, f, 1 - rim).wait_recv()
            fwd_copy(slot, f, rim).start()

        each_side(act)

    def wait_rims(slot, f):
        each_side(lambda rim, _: fwd_copy(slot, f, rim).wait_recv())

    def add(slot, f, ref_of, times, row, taps):
        lo, hi = taps
        group, span = 3 * depth, CORES * depth
        product = lax.dot_general(
            jnp.concatenate([ref_of(f + t, c) for t in times for c in range(CORES)], axis=1),
            wt[slot, times[0] * span : (times[-1] + 1) * span, lo * group : (hi + 1) * group],
            (((1,), (0,)), ((), ())),
            preferred_element_type=jnp.float32,
        )
        for i in range(lo, hi + 1):
            start = (f * row_count + row + 1 - i) * width
            at = pl.ds(start if isinstance(row, int) else pl.multiple_of(start, width), width)
            acc[at, :] = acc[at, :] + product[:, (i - lo) * group : (i - lo + 1) * group]

    every = (0, 1, 2)

    def add_row(slot, f, row, taps, times=every):
        start = row * width
        at = pl.ds(start if isinstance(row, int) else pl.multiple_of(start, width), width)
        add(slot, f, lambda g, c: xb[slot, g, c, at, :], times, row, taps)

    def add_edges(slot, f):
        add_row(slot, f, 0, (0, 1))
        add_row(slot, f, row_count - 1, (1, 2))

    def add_middle(slot, f, times=every):
        pl.loop(1, row_count - 1)(lambda row: add_row(slot, f, row, (0, 2), times))

    def add_rims(slot, f, times=every):
        for rim, row in ((0, -1), (1, row_count)):
            add(
                slot, f, lambda g, c, rim=rim: hb[slot, rim, g, c], times,
                row, (2 * rim, 2 * rim),
            )

    def finish(f):
        column = lax.broadcasted_iota(jnp.int32, (width, depth), 0)

        @pl.loop(0, row_count)
        def _(row):
            at = pl.ds(pl.multiple_of((f * row_count + row) * width, width), width)
            left = pltpu.roll(acc[at, 0:depth], 1, 0)
            right = pltpu.roll(acc[at, 2 * depth : 3 * depth], width - 1, 0)
            total = acc[at, depth : 2 * depth]
            total = total + jnp.where(column == 0, 0.0, left)
            total = total + jnp.where(column == width - 1, 0.0, right)
            obuf[f, pl.ds(pl.multiple_of(row * width, width), width), :] = total.astype(obuf.dtype)

        out_copy(f).start()

    def out_copy(f):
        return pltpu.make_async_copy(obuf.at[f], out_ref.at[f], out_sem.at[f])

    others = range(1, chips)

    def wait_sibling(f, parts):
        for step in others:
            for part in parts:
                sib_copy(step, f, part).wait_recv()

    turn_weights(0)
    for f in range(outs):
        for g in range(3) if f == 0 else (f + 2,):
            local_copy(g).wait()
            own_copy(g).wait_recv()
        add_edges(0, f)
        add_middle(0, f)
        serve(f)
    for slot in others:
        turn_weights(slot)
    for place in range(outs, frames):
        serve(place)
    for f in range(frames):
        serve_edges(0, f)
        wait_sibling(f, (FIRST, LAST))
    for f in range(outs):
        for step in others:
            add_edges(step, f)
        if f % 2 == 1:
            serve(frames + f // 2)
    for f in range(frames):
        wait_rims(0, f)
    for f in range(outs):
        add_rims(0, f)
    for f in range(2, frames):
        serve(frames + f)
        last = f == frames - 1
        for step in others:
            for g in (0, 1, 2) if f == 2 else (f,):
                serve_edges(step, g)
        for g in (0, 1, 2) if f == 2 else (f,):
            wait_sibling(g, (MIDDLE,))
        for step in others:
            add_middle(step, f - 2, (2,) if last else every)
            for g in (0, 1, 2) if f == 2 else (f,):
                wait_rims(step, g)
            add_rims(step, f - 2, (2,) if last else every)
        finish(f - 2)
        if f == frames - 2:
            for step in others:
                add_middle(step, outs - 1, (0, 1))
                add_rims(step, outs - 1, (0, 1))

    for f in range(frames):
        own_copy(f).wait_send()
        for slot in range(chips):
            for part in range(3) if slot > 0 else ():
                sib_copy(slot, f, part).wait_send()

            def gone(side, _, slot=slot, f=f):
                edge_copy(slot, f, side).wait_send()
                fwd_copy(slot, f, side).wait_send()

            each_side(gone)
    for f in range(outs):
        out_copy(f).wait()


def copy_kernel(src_ref, dst_ref, sems):
    copies = [
        pltpu.make_async_copy(src_ref.at[f], dst_ref.at[f], sems.at[f])
        for f in range(src_ref.shape[0])
    ]
    for copy in copies:
        copy.start()
    for copy in copies:
        copy.wait()


def on_device(bands, chans, new_frames, cached_frames, conv_weight, out_bias):
    outs, row_count, own_depth, width = new_frames.shape
    cached = cached_frames.shape[0]
    frames = cached + outs
    chips = chans // CORES
    depth = -(-own_depth // LANES) * LANES
    extra = depth - own_depth

    def rows_first(block):
        block = block.transpose(0, 1, 3, 2).reshape(block.shape[0], row_count * width, own_depth)
        return jnp.pad(block, ((0, 0), (0, 0), (0, extra)))

    weights = conv_weight.reshape(3, 9, own_depth, chans, own_depth)
    weights = jnp.pad(weights, ((0, 0), (0, 0), (0, extra), (0, 0), (0, extra)))
    weights = weights.reshape(3, 9 * depth, chans * depth)
    dims = (bands, chans, cached, outs, depth, width, row_count)
    sem = pltpu.SemaphoreType.DMA
    positions = row_count * width
    result = pl.pallas_call(
        functools.partial(conv_kernel, dims),
        out_shape=jax.ShapeDtypeStruct((outs, positions, depth), jnp.bfloat16),
        in_specs=[
            pl.BlockSpec(memory_space=pl.ANY),
            pl.BlockSpec(memory_space=pl.ANY),
            pl.BlockSpec(memory_space=pl.ANY),
            pl.BlockSpec(memory_space=pltpu.VMEM),
        ],
        out_specs=pl.BlockSpec(memory_space=pl.ANY),
        scratch_shapes=[
            pltpu.VMEM((chips, frames, CORES, positions, depth), jnp.bfloat16),
            pltpu.VMEM((chips, 2, frames, CORES, width, depth), jnp.bfloat16),
            pltpu.VMEM((chips, 9 * depth, 3 * CORES * depth), jnp.bfloat16),
            pltpu.VMEM((chips, 3 * CORES * depth, 9 * depth), jnp.bfloat16),
            pltpu.VMEM((outs * positions, 3 * depth), jnp.float32),
            pltpu.VMEM((outs, positions, depth), jnp.bfloat16),
            sem((frames,)),
            sem((chips, 3)),
            sem((outs,)),
            sem((chips, 3, frames)),
            sem((chips, 3, frames)),
            sem((chips, 3, frames)),
            sem((chips, 3, frames)),
            sem((chips, 2, frames)),
            sem((chips, 2, frames)),
            sem((chips, 2, frames)),
            sem((chips, 2, frames)),
        ],
        compiler_params=pltpu.CompilerParams(
            collective_id=0, has_side_effects=True, vmem_limit_bytes=56 * 2**20
        ),
        cost_estimate=pl.CostEstimate(
            flops=2 * 27 * outs * positions * depth * chans * depth,
            bytes_accessed=2 * (weights.size + (frames + outs) * positions * depth),
            transcendentals=0,
        ),
    )(
        rows_first(cached_frames), rows_first(new_frames), weights,
        jnp.pad(out_bias, (0, extra))[None, :],
    )
    result = pl.pallas_call(
        copy_kernel,
        out_shape=jax.ShapeDtypeStruct(result.shape, result.dtype),
        in_specs=[pl.BlockSpec(memory_space=pl.ANY)],
        out_specs=pl.BlockSpec(memory_space=pl.ANY),
        scratch_shapes=[sem((outs,))],
        cost_estimate=pl.CostEstimate(
            flops=0, bytes_accessed=4 * result.size, transcendentals=0
        ),
    )(result)
    result = result[:, :, :own_depth].reshape(outs, row_count, width, own_depth)
    return result.transpose(0, 1, 3, 2)


def solution(mesh):
    in_specs = (
        P(None, "band", "chan", None),
        P(None, "band", "chan", None),
        P(None, None, None, "chan", None),
        P("chan"),
    )
    out_specs = P(None, "band", "chan", None)
    return jax.shard_map(
        functools.partial(on_device, mesh.shape["band"], mesh.shape["chan"]),
        mesh=mesh, in_specs=in_specs, out_specs=out_specs, check_vma=False,
    )
```

```python
import functools

import jax
import jax.numpy as jnp
from jax import lax
from jax.experimental import pallas as pl
from jax.experimental.pallas import tpu as pltpu
from jax.sharding import PartitionSpec as P

MESH = pl.DeviceIdType.MESH
LANES = 128
CORES = 2


def conv_kernel(
    dims, cached_ref, new_ref, w_ref, bias_ref, out_ref,
    xb, wb, wt, acc, rim_out, rim_in, obuf,
    local_sem, weight_sem, out_sem,
    peer_send, peer_recv, sib_send, sib_recv,
    rim_send, rim_recv,
):
    bands, chans, cached, outs, depth, width, row_count = dims
    frames = cached + outs
    chips = chans // CORES
    band, chan = lax.axis_index("band"), lax.axis_index("chan")
    chip, core = chan // CORES, chan % CORES
    sibling = {"chan": chip * CORES + (1 - core)}
    has_above, has_below = band > 0, band < bands - 1
    sides = ((0, has_above, {"band": band - 1}), (1, has_below, {"band": band + 1}))

    def peer(step):
        return {"chan": lax.rem(chip + step, chips) * CORES + core}

    def turn_weights(slot):
        for t in range(3):
            weight_copy(slot, t).wait()

        @pl.loop(0, 9)
        def _(n):
            at = pl.ds(pl.multiple_of(n * depth, depth), depth)
            wt[slot, :, at] = wb[slot, at, :].T

    def own(f):
        return cached_ref.at[f] if f < cached else new_ref.at[f - cached]

    def remote(src, dst, send, recv, device):
        return pltpu.make_async_remote_copy(
            src_ref=src, dst_ref=dst, send_sem=send, recv_sem=recv,
            device_id=device, device_id_type=MESH,
        )

    def weight_copy(slot, t):
        owner = lax.rem(chip + chips - slot, chips)
        span = CORES * depth
        return pltpu.make_async_copy(
            w_ref.at[t, :, pl.ds(pl.multiple_of(owner * span, LANES), span)],
            wb.at[slot, :, pl.ds(t * span, span)],
            weight_sem.at[slot, t],
        )

    def local_copy(f):
        return pltpu.make_async_copy(own(f), xb.at[0, f, core], local_sem.at[f])

    FIRST, LAST, MIDDLE = range(3)
    spans = (
        pl.ds(0, width),
        pl.ds((row_count - 1) * width, width),
        pl.ds(width, (row_count - 2) * width),
    )

    def peer_copy(step, f, part):
        return remote(
            own(f).at[spans[part]], xb.at[step, f, core, spans[part]],
            peer_send.at[step, part, f], peer_recv.at[step, part, f], peer(step),
        )

    def own_copy(f):
        return remote(
            own(f), xb.at[0, f, core], sib_send.at[0, 0, f], sib_recv.at[0, 0, f], sibling
        )

    def sib_copy(step, f, part):
        ref = xb.at[step, f, core, spans[part]]
        return remote(ref, ref, sib_send.at[step, part, f], sib_recv.at[step, part, f], sibling)

    def rim_copy(f, side):
        return remote(
            rim_out.at[side, f], rim_in.at[1 - side, f],
            rim_send.at[side, f], rim_recv.at[1 - side, f], sides[side][2],
        )

    def each_side(act):
        for side, there, device in sides:
            pl.when(there)(functools.partial(act, side, device))

    barrier = pltpu.get_barrier_semaphore()

    def greet(device):
        pl.semaphore_signal(barrier, inc=1, device_id=device, device_id_type=MESH)

    greet(sibling)
    for step in range(1, chips):
        greet(peer(step))
    each_side(lambda _, device: greet(device))
    for slot in range(chips):
        for t in range(3):
            weight_copy(slot, t).start()
    for f in range(frames):
        local_copy(f).start()
    pl.semaphore_wait(barrier, chips + has_above.astype(jnp.int32) + has_below.astype(jnp.int32))

    ahead = 4
    queue = [(f, (FIRST, LAST)) for f in range(frames)] + [(f, (MIDDLE,)) for f in range(frames)]

    def send(place):
        f, parts = queue[place]
        for step in range(1, chips):
            for part in parts:
                peer_copy(step, f, part).start()

    for place in range(ahead):
        send(place)
    for f in range(frames):
        own_copy(f).start()
    for rim, there, _ in sides:
        @pl.when(jnp.logical_not(there))
        def _(rim=rim):
            rim_in[rim] = jnp.zeros(rim_in.shape[1:], rim_in.dtype)

    sum_rows = row_count + 2

    @pl.loop(0, outs * sum_rows)
    def _(n):
        at = pl.ds(pl.multiple_of(n * width, width), width)
        acc[at, :] = jnp.zeros((width, 3 * depth), acc.dtype)

    def serve(place):
        f, parts = queue[place]
        for step in range(1, chips):
            for part in parts:
                peer_copy(step, f, part).wait_recv()
                sib_copy(step, f, part).start()
        for step in range(1, chips):
            for part in parts:
                peer_copy(step, f, part).wait_send()
        if place + ahead < len(queue):
            send(place + ahead)

    every = (0, 1, 2)

    def add_row(slot, f, row, times):
        group, span = 3 * depth, CORES * depth
        at = pl.ds(pl.multiple_of(row * width, width), width)
        product = jnp.dot(
            jnp.concatenate(
                [xb[slot, f + t, c, at, :] for t in times for c in range(CORES)], axis=1
            ),
            wt[slot, times[0] * span : (times[-1] + 1) * span, :],
            preferred_element_type=jnp.float32,
        )
        for i in range(3):
            start = (f * sum_rows + row + 2 - i) * width
            to = pl.ds(pl.multiple_of(start, width), width)
            acc[to, :] = acc[to, :] + product[:, i * group : (i + 1) * group]

    def add_edges(slot, f):
        pl.loop(0, 2)(lambda n: add_row(slot, f, n * (row_count - 1), every))

    def add_middle(slot, f, times=every):
        pl.loop(1, row_count - 1)(lambda row: add_row(slot, f, row, times))

    column = lax.broadcasted_iota(jnp.int32, (width, depth), 0)

    def row_sum(f, row):
        at = pl.ds(pl.multiple_of((f * sum_rows + row) * width, width), width)
        left = pltpu.roll(acc[at, 0:depth], 1, 0)
        right = pltpu.roll(acc[at, 2 * depth : 3 * depth], width - 1, 0)
        total = acc[at, depth : 2 * depth] + jnp.where(column == 0, 0.0, left)
        return total + jnp.where(column == width - 1, 0.0, right)

    def send_rims(f):
        def act(side, _):
            rim_out[side, f] = row_sum(f, side * (sum_rows - 1))
            rim_copy(f, side).start()

        each_side(act)

    def finish(f):
        each_side(lambda rim, _: rim_copy(f, 1 - rim).wait_recv())

        def write(row, total):
            at = pl.ds(pl.multiple_of(row * width, width), width)
            obuf[f, at, :] = (total + bias_ref[...]).astype(obuf.dtype)

        @pl.loop(0, 2)
        def _(rim):
            row = rim * (row_count - 1)
            write(row, row_sum(f, row + 1) + rim_in[rim, f])

        @pl.loop(1, row_count - 1)
        def _(row):
            write(row, row_sum(f, row + 1))

        out_copy(f).start()

    def out_copy(f):
        return pltpu.make_async_copy(obuf.at[f], out_ref.at[f], out_sem.at[f])

    others = range(1, chips)

    def wait_sibling(f, parts):
        for step in others:
            for part in parts:
                sib_copy(step, f, part).wait_recv()

    turn_weights(0)
    for f in range(outs):
        for g in range(3) if f == 0 else (f + 2,):
            local_copy(g).wait()
            own_copy(g).wait_recv()
        add_edges(0, f)
        if f % 2 == 1:
            serve(f // 2)
    for slot in others:
        turn_weights(slot)
    for f in range(outs):
        add_middle(0, f)
        serve(f + 2)
        for g in (0, 1, 2) if f == 0 else (f + 2,):
            wait_sibling(g, (FIRST, LAST))
        for step in others:
            add_edges(step, f)
        send_rims(f)
    serve(frames)
    serve(frames + 1)
    for f in range(outs):
        if f == outs - 1:
            for step in others:
                add_middle(step, f, (0, 1))
        serve(frames + f + 2)
        for g in (0, 1, 2) if f == 0 else (f + 2,):
            wait_sibling(g, (MIDDLE,))
        for step in others:
            add_middle(step, f, (2,) if f == outs - 1 else every)
        finish(f)

    for f in range(frames):
        own_copy(f).wait_send()
        for slot in range(chips):
            for part in range(3) if slot > 0 else ():
                sib_copy(slot, f, part).wait_send()
    for f in range(outs):
        each_side(lambda side, _, f=f: rim_copy(f, side).wait_send())
        out_copy(f).wait()


def on_device(bands, chans, new_frames, cached_frames, conv_weight, out_bias):
    outs, row_count, own_depth, width = new_frames.shape
    cached = cached_frames.shape[0]
    frames = cached + outs
    chips = chans // CORES
    depth = -(-own_depth // LANES) * LANES
    extra = depth - own_depth

    def rows_first(block):
        block = block.transpose(0, 1, 3, 2).reshape(block.shape[0], row_count * width, own_depth)
        return jnp.pad(block, ((0, 0), (0, 0), (0, extra)))

    weights = conv_weight.reshape(3, 9, own_depth, chans, own_depth)
    weights = jnp.pad(weights, ((0, 0), (0, 0), (0, extra), (0, 0), (0, extra)))
    weights = weights.reshape(3, 9 * depth, chans * depth)
    dims = (bands, chans, cached, outs, depth, width, row_count)
    sem = pltpu.SemaphoreType.DMA
    positions = row_count * width
    result = pl.pallas_call(
        functools.partial(conv_kernel, dims),
        out_shape=jax.ShapeDtypeStruct((outs, positions, depth), jnp.bfloat16),
        in_specs=[
            pl.BlockSpec(memory_space=pl.ANY),
            pl.BlockSpec(memory_space=pl.ANY),
            pl.BlockSpec(memory_space=pl.ANY),
            pl.BlockSpec(memory_space=pltpu.VMEM),
        ],
        out_specs=pl.BlockSpec(memory_space=pl.ANY),
        scratch_shapes=[
            pltpu.VMEM((chips, frames, CORES, positions, depth), jnp.bfloat16),
            pltpu.VMEM((chips, 9 * depth, 3 * CORES * depth), jnp.bfloat16),
            pltpu.VMEM((chips, 3 * CORES * depth, 9 * depth), jnp.bfloat16),
            pltpu.VMEM((outs * (positions + 2 * width), 3 * depth), jnp.float32),
            pltpu.VMEM((2, outs, width, depth), jnp.float32),
            pltpu.VMEM((2, outs, width, depth), jnp.float32),
            pltpu.VMEM((outs, positions, depth), jnp.bfloat16),
            sem((frames,)),
            sem((chips, 3)),
            sem((outs,)),
            sem((chips, 3, frames)),
            sem((chips, 3, frames)),
            sem((chips, 3, frames)),
            sem((chips, 3, frames)),
            sem((2, outs)),
            sem((2, outs)),
        ],
        compiler_params=pltpu.CompilerParams(
            collective_id=0, has_side_effects=True, vmem_limit_bytes=56 * 2**20
        ),
        cost_estimate=pl.CostEstimate(
            flops=2 * 27 * outs * positions * depth * chans * depth,
            bytes_accessed=2 * (weights.size + (frames + outs) * positions * depth),
            transcendentals=0,
        ),
    )(
        rows_first(cached_frames), rows_first(new_frames), weights,
        jnp.pad(out_bias, (0, extra))[None, :],
    )
    result = result[:, :, :own_depth].reshape(outs, row_count, width, own_depth)
    return result.transpose(0, 1, 3, 2)


def solution(mesh):
    in_specs = (
        P(None, "band", "chan", None),
        P(None, "band", "chan", None),
        P(None, None, None, "chan", None),
        P("chan"),
    )
    out_specs = P(None, "band", "chan", None)
    return jax.shard_map(
        functools.partial(on_device, mesh.shape["band"], mesh.shape["chan"]),
        mesh=mesh, in_specs=in_specs, out_specs=out_specs, check_vma=False,
    )
```

```python
import functools

import jax
import jax.numpy as jnp
from jax import lax
from jax.experimental import pallas as pl
from jax.experimental.pallas import tpu as pltpu
from jax.sharding import PartitionSpec as P

MESH = pl.DeviceIdType.MESH
LANES = 128
CORES = 2


def conv_kernel(
    dims, cached_ref, new_ref, w_ref, bias_ref, out_ref,
    xb, wb, wt, acc, rim_out, rim_in, obuf,
    local_sem, weight_sem, out_sem,
    peer_send, peer_recv, sib_send, sib_recv,
    rim_send, rim_recv,
):
    bands, chans, cached, outs, depth, width, row_count = dims
    frames = cached + outs
    chips = chans // CORES
    band, chan = lax.axis_index("band"), lax.axis_index("chan")
    chip, core = chan // CORES, chan % CORES
    sibling = {"chan": chip * CORES + (1 - core)}
    has_above, has_below = band > 0, band < bands - 1
    sides = ((0, has_above, {"band": band - 1}), (1, has_below, {"band": band + 1}))

    def peer(step):
        return {"chan": lax.rem(chip + step, chips) * CORES + core}

    def turn_weights(slot):
        for t in range(3):
            weight_copy(slot, t).wait()

        @pl.loop(0, 9)
        def _(n):
            at = pl.ds(pl.multiple_of(n * depth, depth), depth)
            wt[slot, :, at] = wb[slot, at, :].T

    def own(f):
        return cached_ref.at[f] if f < cached else new_ref.at[f - cached]

    def remote(src, dst, send, recv, device):
        return pltpu.make_async_remote_copy(
            src_ref=src, dst_ref=dst, send_sem=send, recv_sem=recv,
            device_id=device, device_id_type=MESH,
        )

    def weight_copy(slot, t):
        owner = lax.rem(chip + chips - slot, chips)
        span = CORES * depth
        return pltpu.make_async_copy(
            w_ref.at[t, :, pl.ds(pl.multiple_of(owner * span, LANES), span)],
            wb.at[slot, :, pl.ds(t * span, span)],
            weight_sem.at[slot, t],
        )

    def local_copy(f):
        return pltpu.make_async_copy(own(f), xb.at[0, f, core], local_sem.at[f])

    FIRST, LAST, MIDDLE = range(3)
    spans = (
        pl.ds(0, width),
        pl.ds((row_count - 1) * width, width),
        pl.ds(width, (row_count - 2) * width),
    )

    def peer_copy(step, f, part):
        return remote(
            own(f).at[spans[part]], xb.at[step, f, core, spans[part]],
            peer_send.at[step, part, f], peer_recv.at[step, part, f], peer(step),
        )

    def own_copy(f):
        return remote(
            own(f), xb.at[0, f, core], sib_send.at[0, 0, f], sib_recv.at[0, 0, f], sibling
        )

    def sib_copy(step, f, part):
        ref = xb.at[step, f, core, spans[part]]
        return remote(ref, ref, sib_send.at[step, part, f], sib_recv.at[step, part, f], sibling)

    def rim_copy(f, side):
        return remote(
            rim_out.at[side, f], rim_in.at[1 - side, f],
            rim_send.at[side, f], rim_recv.at[1 - side, f], sides[side][2],
        )

    def each_side(act):
        for side, there, device in sides:
            pl.when(there)(functools.partial(act, side, device))

    barrier = pltpu.get_barrier_semaphore()

    def greet(device):
        pl.semaphore_signal(barrier, inc=1, device_id=device, device_id_type=MESH)

    greet(sibling)
    for step in range(1, chips):
        greet(peer(step))
    each_side(lambda _, device: greet(device))
    for slot in range(chips):
        for t in range(3):
            weight_copy(slot, t).start()
    for f in range(frames):
        local_copy(f).start()
    pl.semaphore_wait(barrier, chips + has_above.astype(jnp.int32) + has_below.astype(jnp.int32))

    ahead = 4
    queue = [(f, (FIRST, LAST)) for f in range(frames)] + [(f, (MIDDLE,)) for f in range(frames)]

    def send(place):
        f, parts = queue[place]
        for step in range(1, chips):
            for part in parts:
                peer_copy(step, f, part).start()

    for place in range(ahead):
        send(place)
    for f in range(frames):
        own_copy(f).start()
    for rim, there, _ in sides:
        @pl.when(jnp.logical_not(there))
        def _(rim=rim):
            rim_in[rim] = jnp.zeros(rim_in.shape[1:], rim_in.dtype)

    sum_rows = row_count + 2

    @pl.loop(0, outs * sum_rows)
    def _(n):
        at = pl.ds(pl.multiple_of(n * width, width), width)
        acc[at, :] = jnp.zeros((width, 3 * depth), acc.dtype)

    def serve(place):
        f, parts = queue[place]
        for step in range(1, chips):
            for part in parts:
                peer_copy(step, f, part).wait_recv()
                sib_copy(step, f, part).start()
        for step in range(1, chips):
            for part in parts:
                peer_copy(step, f, part).wait_send()
        if place + ahead < len(queue):
            send(place + ahead)

    every = (0, 1, 2)

    def add_row(slot, f, row, times):
        group, span = 3 * depth, CORES * depth
        at = pl.ds(pl.multiple_of(row * width, width), width)
        product = jnp.dot(
            jnp.concatenate(
                [xb[slot, f + t, c, at, :] for t in times for c in range(CORES)], axis=1
            ),
            wt[slot, times[0] * span : (times[-1] + 1) * span, :],
            preferred_element_type=jnp.float32,
        )
        for i in range(3):
            start = (f * sum_rows + row + 2 - i) * width
            to = pl.ds(pl.multiple_of(start, width), width)
            acc[to, :] = acc[to, :] + product[:, i * group : (i + 1) * group]

    def add_edges(slot, f):
        pl.loop(0, 2)(lambda n: add_row(slot, f, n * (row_count - 1), every))

    def add_middle(slot, f, times=every):
        pl.loop(1, row_count - 1)(lambda row: add_row(slot, f, row, times))

    column = lax.broadcasted_iota(jnp.int32, (width, depth), 0)

    def row_sum(f, row):
        at = pl.ds(pl.multiple_of((f * sum_rows + row) * width, width), width)
        left = pltpu.roll(acc[at, 0:depth], 1, 0)
        right = pltpu.roll(acc[at, 2 * depth : 3 * depth], width - 1, 0)
        total = acc[at, depth : 2 * depth] + jnp.where(column == 0, 0.0, left)
        return total + jnp.where(column == width - 1, 0.0, right)

    def send_rims(f):
        def act(side, _):
            rim_out[side, f] = row_sum(f, side * (sum_rows - 1))
            rim_copy(f, side).start()

        each_side(act)

    def finish(f):
        each_side(lambda rim, _: rim_copy(f, 1 - rim).wait_recv())

        def write(row, total):
            at = pl.ds(pl.multiple_of(row * width, width), width)
            obuf[f, at, :] = (total + bias_ref[...]).astype(obuf.dtype)

        @pl.loop(0, 2)
        def _(rim):
            row = rim * (row_count - 1)
            write(row, row_sum(f, row + 1) + rim_in[rim, f])

        @pl.loop(1, row_count - 1)
        def _(row):
            write(row, row_sum(f, row + 1))

        out_copy(f).start()

    def out_copy(f):
        return pltpu.make_async_copy(obuf.at[f], out_ref.at[f], out_sem.at[f])

    others = range(1, chips)

    def wait_sibling(f, parts):
        for step in others:
            for part in parts:
                sib_copy(step, f, part).wait_recv()

    turn_weights(0)
    for f in range(outs):
        for g in range(3) if f == 0 else (f + 2,):
            local_copy(g).wait()
            own_copy(g).wait_recv()
        add_edges(0, f)
        if f % 2 == 1:
            serve(f // 2)
    for slot in others:
        turn_weights(slot)
    for f in range(outs):
        add_middle(0, f)
        serve(f + 2)
        for g in (0, 1, 2) if f == 0 else (f + 2,):
            wait_sibling(g, (FIRST, LAST))
        for step in others:
            add_edges(step, f)
        send_rims(f)
    serve(frames)
    serve(frames + 1)
    for f in range(outs):
        if f == outs - 1:
            for step in others:
                add_middle(step, f, (0, 1))
        serve(frames + f + 2)
        for g in (0, 1, 2) if f == 0 else (f + 2,):
            wait_sibling(g, (MIDDLE,))
        for step in others:
            add_middle(step, f, (2,) if f == outs - 1 else every)
        finish(f)

    for f in range(frames):
        own_copy(f).wait_send()
        for slot in range(chips):
            for part in range(3) if slot > 0 else ():
                sib_copy(slot, f, part).wait_send()
    for f in range(outs):
        each_side(lambda side, _, f=f: rim_copy(f, side).wait_send())
        out_copy(f).wait()


def copy_kernel(src_ref, dst_ref):
    dst_ref[...] = src_ref[...]


def on_device(bands, chans, new_frames, cached_frames, conv_weight, out_bias):
    outs, row_count, own_depth, width = new_frames.shape
    cached = cached_frames.shape[0]
    frames = cached + outs
    chips = chans // CORES
    depth = -(-own_depth // LANES) * LANES
    extra = depth - own_depth

    def rows_first(block):
        block = block.transpose(0, 1, 3, 2).reshape(block.shape[0], row_count * width, own_depth)
        return jnp.pad(block, ((0, 0), (0, 0), (0, extra)))

    weights = conv_weight.reshape(3, 9, own_depth, chans, own_depth)
    weights = jnp.pad(weights, ((0, 0), (0, 0), (0, extra), (0, 0), (0, extra)))
    weights = weights.reshape(3, 9 * depth, chans * depth)
    dims = (bands, chans, cached, outs, depth, width, row_count)
    sem = pltpu.SemaphoreType.DMA
    positions = row_count * width
    result = pl.pallas_call(
        functools.partial(conv_kernel, dims),
        out_shape=jax.ShapeDtypeStruct((outs, positions, depth), jnp.bfloat16),
        in_specs=[
            pl.BlockSpec(memory_space=pl.ANY),
            pl.BlockSpec(memory_space=pl.ANY),
            pl.BlockSpec(memory_space=pl.ANY),
            pl.BlockSpec(memory_space=pltpu.VMEM),
        ],
        out_specs=pl.BlockSpec(memory_space=pl.ANY),
        scratch_shapes=[
            pltpu.VMEM((chips, frames, CORES, positions, depth), jnp.bfloat16),
            pltpu.VMEM((chips, 9 * depth, 3 * CORES * depth), jnp.bfloat16),
            pltpu.VMEM((chips, 3 * CORES * depth, 9 * depth), jnp.bfloat16),
            pltpu.VMEM((outs * (positions + 2 * width), 3 * depth), jnp.float32),
            pltpu.VMEM((2, outs, width, depth), jnp.float32),
            pltpu.VMEM((2, outs, width, depth), jnp.float32),
            pltpu.VMEM((outs, positions, depth), jnp.bfloat16),
            sem((frames,)),
            sem((chips, 3)),
            sem((outs,)),
            sem((chips, 3, frames)),
            sem((chips, 3, frames)),
            sem((chips, 3, frames)),
            sem((chips, 3, frames)),
            sem((2, outs)),
            sem((2, outs)),
        ],
        compiler_params=pltpu.CompilerParams(
            collective_id=0, has_side_effects=True, vmem_limit_bytes=56 * 2**20
        ),
        cost_estimate=pl.CostEstimate(
            flops=2 * 27 * outs * positions * depth * chans * depth,
            bytes_accessed=2 * (weights.size + (frames + outs) * positions * depth),
            transcendentals=0,
        ),
    )(
        rows_first(cached_frames), rows_first(new_frames), weights,
        jnp.pad(out_bias, (0, extra))[None, :],
    )
    block = pl.BlockSpec((1, positions, depth), lambda f: (f, 0, 0))
    result = pl.pallas_call(
        copy_kernel,
        out_shape=jax.ShapeDtypeStruct(result.shape, result.dtype),
        grid=(outs,),
        in_specs=[block],
        out_specs=block,
        cost_estimate=pl.CostEstimate(
            flops=0, bytes_accessed=4 * result.size, transcendentals=0
        ),
    )(result)
    result = result[:, :, :own_depth].reshape(outs, row_count, width, own_depth)
    return result.transpose(0, 1, 3, 2)


def solution(mesh):
    in_specs = (
        P(None, "band", "chan", None),
        P(None, "band", "chan", None),
        P(None, None, None, "chan", None),
        P("chan"),
    )
    out_specs = P(None, "band", "chan", None)
    return jax.shard_map(
        functools.partial(on_device, mesh.shape["band"], mesh.shape["chan"]),
        mesh=mesh, in_specs=in_specs, out_specs=out_specs, check_vma=False,
    )
```
